256 devices in a mesh: gx: 8 (over x, core), gy: 32 (over y, z).
Axes of the slice: x: 4, y: 4, z: 8, core: 2. Of those that a mesh axis runs over, the one named last changes fastest.
Arguments:
- span: float32 [524288, 256], P(('gx', 'gy')), as said below
- prior: float32 [256, 256], replicated, as said below
- counts: int32 [256], P(('gx', 'gy')), may hold values from 128 to 2048, as said below
Outputs:
- r_scaled: float32 [256, 256], replicated
- q_scaled: float32 [524288, 256], P(('gx', 'gy'))
The draws below stay inside these ranges and needn't reach their ends.
Inputs may be any that keep to these rules, and one draw needn't show every extreme that they name: counts[d] is the number of live rows at the start of device block d; at least one block is full. prior is upper triangular with a positive diagonal. `span`: rows that are not live hold arbitrary values.
All inputs are finite; a program needn't handle non-finite values.
Results may differ from the reference program's by a relative error of at most 0.0003.
Values sent between devices are 32-bit elements; how exact they have to be, the bound alone decides.
No kernel may reach another device: no remote copies, remote signals or barrier semaphores. Data moves between devices by JAX's collectives and lax.ppermute only.
A program may use at most 64 MiB of HBM per device.

```python
import math
import jax
import jax.numpy as jnp
from jax import lax

C = 256
ROW_DEV = 2048
ROWS = 524288


def column_law(key):
    base_key = jax.random.fold_in(key, 3)
    key_scale, key_mix, key_sign, key_gap = jax.random.split(base_key, 4)
    col_scales = jnp.exp(jax.random.uniform(key_scale, (C,), jnp.float32, 0.0, math.log(10.0)))
    sign_vals = (2 * jax.random.randint(key_sign, (C,), 0, 2) - 1).astype(jnp.float32)
    mix_coef = jax.random.uniform(key_mix, (C,), jnp.float32, 0.5, 1.5) * sign_vals
    gap_sizes = jnp.exp(jax.random.uniform(key_gap, (C,), jnp.float32, math.log(0.006), math.log(0.024)))
    return (col_scales, mix_coef, gap_sizes)


def pair_columns(base_vals, key):
    col_scales, mix_coef, gap_sizes = column_law(key)
    shifted = jnp.roll(base_vals, 1, axis=1)
    odd_cols = (jnp.arange(C) % 2 == 1)[None, :]
    paired = jnp.where(odd_cols, mix_coef[None, :] * shifted + gap_sizes[None, :] * base_vals, base_vals)
    return paired * col_scales[None, :]


def draw_span(key, part):
    key_noise, key_rows = jax.random.split(jax.random.fold_in(key, 1), 2)
    devices_all = ROWS // ROW_DEV
    noise_vals = jax.random.normal(key_noise, (ROWS, C), jnp.float32)
    ramp_log = math.log(4.0)
    noise_vals = jnp.clip(noise_vals, -5.0, 5.0)
    row_scales = jnp.exp(jax.random.uniform(key_rows, (ROWS, 1), jnp.float32, 0.0, math.log(10.0)))
    device_of = jnp.arange(ROWS) // ROW_DEV
    device_ramp = jnp.exp(ramp_log * device_of.astype(jnp.float32) / max(devices_all - 1, 1))[:, None]
    spiked = jnp.where((device_of % C)[:, None] == jnp.arange(C)[None, :], 3.0, 1.0)
    base_vals = 0.1 * noise_vals * row_scales * device_ramp * spiked
    return pair_columns(base_vals, key)


def draw_prior(key, part):
    key_diag, key_off = jax.random.split(jax.random.fold_in(key, 2), 2)
    root_rows = math.sqrt(ROWS)
    diag_vals = 0.3 * jnp.exp(jax.random.uniform(key_diag, (C,), jnp.float32, 0.0, math.log(5.0)))
    off_vals = jnp.clip(jax.random.normal(key_off, (C, C), jnp.float32), -4.0, 4.0)
    row_idx = jnp.arange(C)[:, None]
    col_idx = jnp.arange(C)[None, :]
    strict = jnp.where(col_idx > row_idx, off_vals * (0.6 / math.sqrt(C)), 0.0)
    diag_part = jnp.where(col_idx == row_idx, diag_vals[:, None], 0.0)
    return pair_columns(root_rows * (strict + diag_part), key)


def draw_counts(key, part):
    key_halving, key_bits, key_full = jax.random.split(key, 3)
    devices_all = ROWS // ROW_DEV
    halving = jax.random.randint(key_halving, (devices_all,), 0, 4)
    low_end = jnp.right_shift(ROW_DEV, halving + 1)
    high_end = jnp.right_shift(ROW_DEV, halving)
    raw_bits = jax.random.randint(key_bits, (devices_all,), 0, 1 << 30)
    picked = low_end + raw_bits % (high_end - low_end + 1)
    full_device = jax.random.randint(key_full, (), 0, devices_all)
    return jnp.where(jnp.arange(devices_all) == full_device, ROW_DEV, picked).astype(jnp.int32)


def setup_inputs(seed: int = 0) -> dict:
    seeds = jax.random.split(jax.random.key(seed), 4)
    span = draw_span(jax.random.fold_in(seeds[3], 71), 0)
    prior = draw_prior(jax.random.fold_in(seeds[3], 71), 0)
    counts = draw_counts(jax.random.fold_in(seeds[3], 71), 0)
    return dict(span=span, prior=prior, counts=counts)


def reference(span, prior, counts):
    device_count = ROWS // ROW_DEV
    live_mask = (jnp.arange(ROW_DEV)[None, :] < counts[:, None]).astype(span.dtype)
    masked = (span.reshape(device_count, ROW_DEV, C) * live_mask[:, :, None]).reshape(ROWS, C)
    blocks = lax.map(lambda part_rows: jnp.linalg.qr(part_rows, mode='r'), masked.reshape(device_count, ROW_DEV, C))
    stacked = jnp.concatenate([prior, blocks.reshape(-1, C)], axis=0)
    r_factor = jnp.linalg.qr(stacked, mode='r')
    sign_fix = jnp.where(jnp.diagonal(r_factor) < 0, -1.0, 1.0).astype(r_factor.dtype)
    r_factor = r_factor * sign_fix[:, None]
    root_rows = math.sqrt(ROWS)
    q_scaled = jax.scipy.linalg.solve_triangular(r_factor, masked.T, trans='T', lower=False).T * root_rows
    return (r_factor / root_rows, q_scaled)
```

```python
import functools
import math

import jax
import jax.numpy as jnp
from jax import lax
from jax.experimental import pallas as pl
from jax.experimental.pallas import tpu as pltpu
from jax.sharding import Mesh, PartitionSpec as P

F32 = jnp.float32
exact = lax.Precision.HIGHEST
N = 256
SUB = 8
PANEL = 64


def mm(a, b, dims=((1,), (0,))):
    return lax.dot_general(a, b, (dims, ((), ())), precision=exact, preferred_element_type=F32)


def iota(shape, dim):
    return lax.broadcasted_iota(jnp.int32, shape, dim)


def lane_group_copy(x, k):
    half = x.shape[1] // 128
    out = []
    for h in range(half):
        part = x[:, 128 * h : 128 * (h + 1)]
        idx = (iota(part.shape, 1) // SUB) * SUB + k
        out.append(jnp.take_along_axis(part, idx, axis=1))
    return jnp.concatenate(out, axis=1)


def upper_inverse(p_ref):
    lane = iota((SUB, N), 1)
    sub = iota((SUB, N), 0)
    diag = jnp.zeros((SUB, N), F32)
    for b in range(N // SUB):
        diag = jnp.where(lane // SUB == b, p_ref[SUB * b : SUB * (b + 1), :], diag)
    rest = jnp.where(lane % SUB == sub, 1.0, 0.0)
    small = jnp.zeros((SUB, N), F32)
    for k in reversed(range(SUB)):
        column = lane_group_copy(diag, k)
        row = jnp.broadcast_to(rest[k : k + 1, :] / column[k : k + 1, :], (SUB, N))
        small = jnp.where(sub == k, row, small)
        if k:
            rest = rest - jnp.where(sub < k, column, 0.0) * row
    row_all, col_all = iota((N, N), 0), iota((N, N), 1)
    inverse = jnp.where(row_all // SUB == col_all // SUB, jnp.concatenate([small] * (N // SUB), axis=0), 0.0)
    upper = p_ref[...]
    size = SUB
    while size < N:
        pair = (row_all // (2 * size) == col_all // (2 * size)) & (row_all // size < col_all // size)
        inverse = inverse - mm(inverse, mm(jnp.where(pair, upper, 0.0), inverse))
        size *= 2
    return inverse


def first_kernel(counts_ref, span_ref, prior_ref, y_ref, gram_ref, inverse_ref):
    live = counts_ref[0]
    inverse_ref[...] = upper_inverse(prior_ref)
    block = 512
    gram_ref[...] = jnp.zeros((N, N), F32)
    for b in range(span_ref.shape[0] // block):
        start = b * block

        @pl.when(start < live)
        def _():
            rows = span_ref[start : start + block, :]
            keep = iota((block, N), 0) + start < live
            image = mm(jnp.where(keep, rows, 0.0), inverse_ref[...])
            y_ref[start : start + block, :] = image
            gram_ref[...] += mm(image, image, ((0,), (0,)))

        @pl.when(start >= live)
        def _():
            y_ref[start : start + block, :] = jnp.zeros((block, N), F32)


def eliminate_panel(m_ref, r_ref, p):
    base = p * PANEL
    groups = PANEL // SUB
    lane = iota((SUB, N), 1)
    sub = iota((SUB, N), 0)
    sub1 = iota((SUB, 128), 0)
    for t in range(groups):
        top = base + t * SUB
        cols = []
        for k in range(SUB):
            cols.append([
                jnp.broadcast_to(m_ref[base + g * SUB : base + (g + 1) * SUB, top + k : top + k + 1], (SUB, 128))
                for g in range(t, groups)
            ])
        s = {}
        for k in range(SUB):
            for i in range(k, SUB):
                s[i, k] = jnp.broadcast_to(cols[k][0][i : i + 1, :], (SUB, 128))
        scale = []
        low = {}
        for k in range(SUB):
            r = lax.rsqrt(s[k, k])
            scale.append(r)
            for i in range(k + 1, SUB):
                low[i, k] = s[i, k] * r
            for j in range(k + 1, SUB):
                for i in range(j, SUB):
                    s[i, j] = s[i, j] - low[i, k] * low[j, k]
            for g in range(1, groups - t):
                cols[k][g] = cols[k][g] * r
                for j in range(k + 1, SUB):
                    cols[j][g] = cols[j][g] - cols[k][g] * low[j, k]
        half = top // 128
        own = slice(128 * half, 128 * (half + 1))
        lane_own = iota((SUB, 128), 1) + 128 * half
        rows = []
        twin = []
        for k in range(SUB):
            full = jnp.broadcast_to(m_ref[top + k : top + k + 1, :], (SUB, N))
            part = jnp.where(
                (lane_own >= top) & (lane_own < top + SUB),
                jnp.where(lane_own == top + k, 1.0, 0.0),
                full[:, own],
            )
            for j in range(k):
                c = low[k, j]
                full = full - jnp.concatenate([c, c], axis=1) * rows[j]
                part = part - c * twin[j]
            r = scale[k]
            rows.append(full * jnp.concatenate([r, r], axis=1))
            twin.append(part * r)
        w_true = rows[0]
        w_own = twin[0]
        for k in range(1, SUB):
            w_true = jnp.where(sub == k, rows[k], w_true)
            w_own = jnp.where(sub1 == k, twin[k], w_own)
        r_ref[top : top + SUB, :] = jnp.where(lane >= top + sub, w_true, 0.0)
        w_parts = [w_true[:, :128], w_true[:, 128:]]
        w_parts[half] = w_own
        m_ref[top : top + SUB, :] = jnp.concatenate(w_parts, axis=1)
        for g in range(1, groups - t):
            at = slice(base + (t + g) * SUB, base + (t + g + 1) * SUB)
            for h in range(2):
                old = m_ref[at, 128 * h : 128 * (h + 1)]
                if h == half:
                    old = jnp.where((lane_own >= top) & (lane_own < top + SUB), 0.0, old)
                total = None
                for k in range(SUB):
                    row = twin[k] if h == half else rows[k][:, 128 * h : 128 * (h + 1)]
                    term = cols[k][g] * row
                    total = term if total is None else total + term
                m_ref[at, 128 * h : 128 * (h + 1)] = old - total


def factor(m_ref, r_ref):
    for p in range(N // PANEL):
        eliminate_panel(m_ref, r_ref, p)
        base, below = p * PANEL, (p + 1) * PANEL
        if below < N:
            w = m_ref[base:below, :]
            lane = iota((PANEL, N), 1)
            ahead = (lane < below) & (lane > base + iota((PANEL, N), 0))
            gain = mm(w[:, below:] if below % 128 == 0 else w, jnp.where(ahead, 0.0, w), ((0,), (0,)))
            if below % 128:
                gain = gain[below:, :]
            lane = iota((N - below, N), 1)
            old = jnp.where((lane >= base) & (lane < below), 0.0, m_ref[below:, :])
            m_ref[below:, :] = old - gain


def second_kernel(row_scale, packed_ref, prior_ref, y_ref, r_out, q_out, m_ref, r_ref):
    m_ref[0:64, :] = packed_ref[0:64, :]
    second = packed_ref[64:128, :]
    m_ref[64:128, :] = second
    m_ref[128:160, 128:256] = packed_ref[128:160, 128:256]
    m_ref[160:192, 128:256] = packed_ref[128:160, 0:128]
    m_ref[192:256, 128:256] = pltpu.roll(second[:, 0:128], 64, 1)
    m_ref[128:256, 0:128] = jnp.zeros((128, 128), F32)
    row_all, col_all = iota((N, N), 0), iota((N, N), 1)
    m_ref[...] = jnp.where(
        row_all // PANEL <= col_all // PANEL,
        m_ref[...] + jnp.where(row_all == col_all, 1.0, 0.0),
        0.0,
    )
    factor(m_ref, r_ref)
    r_out[...] = mm(r_ref[...], prior_ref[...]) * (1.0 / row_scale)
    low_inverse = jnp.where(row_all >= col_all, m_ref[...], 0.0) * row_scale
    r_ref[...] = low_inverse
    block = 512
    for b in range(y_ref.shape[0] // block):
        at = slice(b * block, (b + 1) * block)
        q_out[at, :] = mm(y_ref[at, :], r_ref[...], ((1,), (1,)))


def swap(value, axis, pairs):
    return lax.ppermute(value, axis, [p for a, b in pairs for p in ((a, b), (b, a))])


RING4 = (((0, 1), (2, 3)), ((1, 2), (3, 0)))
RING8 = (((0, 1), (2, 3), (4, 5), (6, 7)), ((1, 2), (3, 4), (5, 6), (7, 0)), ((0, 3), (1, 6), (2, 5), (4, 7)))


def sum_all(packed):
    one = lax.axis_index("core") == 1
    half = packed.shape[0] // 2
    first, last = packed[:half], packed[half:]
    mine = jnp.where(one, last, first) + swap(jnp.where(one, first, last), "core", ((0, 1),))
    for axis, turns in (("x", RING4), ("y", RING4), ("z", RING8)):
        for pairs in turns:
            mine = mine + swap(mine, axis, pairs)
    other = swap(mine, "core", ((0, 1),))
    return jnp.concatenate([jnp.where(one, other, mine), jnp.where(one, mine, other)], axis=0)


def pack(gram):
    lane = iota((64, N), 1)
    second = jnp.where(lane < 64, jnp.roll(gram[192:256, :], 64, axis=1), gram[64:128, :])
    third = jnp.concatenate([gram[160:192, 128:256], gram[128:160, 128:256]], axis=1)
    return jnp.concatenate([gram[0:64, :], second, third], axis=0)


VMEM = pl.BlockSpec(memory_space=pltpu.VMEM)
SMEM = pl.BlockSpec(memory_space=pltpu.SMEM)
PARAMS = pltpu.CompilerParams(vmem_limit_bytes=40 * 2**20)


def stage_one(span, prior, counts):
    rows = span.shape[0]
    return pl.pallas_call(
        first_kernel,
        out_shape=(jax.ShapeDtypeStruct((rows, N), F32), jax.ShapeDtypeStruct((N, N), F32)),
        in_specs=[SMEM, VMEM, VMEM],
        out_specs=(VMEM, VMEM),
        scratch_shapes=[pltpu.VMEM((N, N), F32)],
        compiler_params=PARAMS,
    )(counts, span, prior)


def stage_two(packed, prior, y, row_scale):
    rows = y.shape[0]
    return pl.pallas_call(
        functools.partial(second_kernel, row_scale),
        out_shape=(jax.ShapeDtypeStruct((N, N), F32), jax.ShapeDtypeStruct((rows, N), F32)),
        in_specs=[VMEM, VMEM, VMEM],
        out_specs=(VMEM, VMEM),
        scratch_shapes=[pltpu.VMEM((N, N), F32), pltpu.VMEM((N, N), F32)],
        compiler_params=PARAMS,
    )(packed, prior, y)


def per_device(span, prior, counts, row_scale):
    y, gram = stage_one(span, prior, counts)
    return stage_two(sum_all(pack(gram)), prior, y, row_scale)


def solution(mesh):
    fine = Mesh(mesh.devices.reshape(4, 2, 4, 8), ("x", "core", "y", "z"))
    split = ("x", "core", "y", "z")

    def run(span, prior, counts):
        row_scale = math.sqrt(span.shape[0])
        return jax.shard_map(
            functools.partial(per_device, row_scale=row_scale),
            mesh=fine,
            in_specs=(P(split, None), P(), P(split)),
            out_specs=(P(), P(split, None)),
            check_vma=False,
        )(span, prior, counts)

    return run
```

```python
import functools
import math

import jax
import jax.numpy as jnp
from jax import lax
from jax.experimental import pallas as pl
from jax.experimental.pallas import tpu as pltpu
from jax.sharding import Mesh, PartitionSpec as P

F32 = jnp.float32
BF16 = jnp.bfloat16
BLOCK = 512
exact = lax.Precision.HIGHEST
N = 256
SUB = 8
PANEL = 64


def mm(a, b, dims=((1,), (0,))):
    return lax.dot_general(a, b, (dims, ((), ())), precision=exact, preferred_element_type=F32)


def cut(x, parts):
    out = []
    for _ in range(parts):
        out.append(x.astype(BF16))
        x = x - out[-1].astype(F32)
    return out


def dot(a, b, dims=((1,), (0,))):
    return lax.dot_general(a, b, (dims, ((), ())), preferred_element_type=F32)


def mm6(left, right):
    a1, a2, a3 = left
    b1, b2, b3 = right
    return dot(jnp.concatenate([a3, a2, a1, a2, a1, a1], axis=1), jnp.concatenate([b1, b2, b3, b1, b2, b1], axis=0))


def iota(shape, dim):
    return lax.broadcasted_iota(jnp.int32, shape, dim)


def lane_group_copy(x, k):
    half = x.shape[1] // 128
    out = []
    for h in range(half):
        part = x[:, 128 * h : 128 * (h + 1)]
        idx = (iota(part.shape, 1) // SUB) * SUB + k
        out.append(jnp.take_along_axis(part, idx, axis=1))
    return jnp.concatenate(out, axis=1)


def small_inverses(p_ref):
    lane = iota((SUB, N), 1)
    sub = iota((SUB, N), 0)
    diag = jnp.zeros((SUB, N), F32)
    for b in range(N // SUB):
        diag = jnp.where(lane // SUB == b, p_ref[SUB * b : SUB * (b + 1), :], diag)
    rest = jnp.where(lane % SUB == sub, 1.0, 0.0)
    small = jnp.zeros((SUB, N), F32)
    for k in reversed(range(SUB)):
        column = lane_group_copy(diag, k)
        row = jnp.broadcast_to(rest[k : k + 1, :] / column[k : k + 1, :], (SUB, N))
        small = jnp.where(sub == k, row, small)
        if k:
            rest = rest - jnp.where(sub < k, column, 0.0) * row
    return small


def upper_inverse(p_ref, small):
    half = N // 2
    row, col = iota((half, half), 0), iota((half, half), 1)
    corners = []
    for h in range(2):
        part = slice(half * h, half * (h + 1))
        inverse = jnp.where(row // SUB == col // SUB, jnp.concatenate([small[:, part]] * (half // SUB), axis=0), 0.0)
        upper = p_ref[part, part]
        size = SUB
        while size < half:
            pair = (row // (2 * size) == col // (2 * size)) & (row // size < col // size)
            known = cut(inverse, 3)
            inverse = inverse - mm6(known, cut(mm6(cut(jnp.where(pair, upper, 0.0), 3), known), 3))
            size *= 2
        corners.append(inverse)
    known = [cut(c, 3) for c in corners]
    cross = mm6(known[0], cut(mm6(cut(p_ref[:half, half:], 3), known[1]), 3))
    top = jnp.concatenate([corners[0], -cross], axis=1)
    return jnp.concatenate([top, jnp.concatenate([jnp.zeros((half, half), F32), corners[1]], axis=1)], axis=0)


def first_kernel(
    counts_ref, span_ref, prior_ref, high_out, low_out, packed_ref, rows_ref, parts_ref, high_ref, low_ref, in_sems, out_sems
):
    live = counts_ref[0]
    count = span_ref.shape[0] // BLOCK
    blocks = [pl.ds(b * BLOCK, BLOCK) for b in range(count)]
    copies = [pltpu.make_async_copy(span_ref.at[at, :], rows_ref.at[at, :], in_sems.at[b]) for b, at in enumerate(blocks)]
    for copy in copies:
        copy.start()
    small = small_inverses(prior_ref)
    for copy in copies:
        copy.wait()
    for b, at in enumerate(blocks):
        keep = iota((BLOCK, N), 0) + b * BLOCK < live
        for i, part in enumerate(cut(jnp.where(keep, rows_ref[at, :], 0.0), 3)):
            parts_ref[at, i * N : (i + 1) * N] = part
    b1, b2, b3 = cut(upper_inverse(prior_ref, small), 3)
    right = jnp.concatenate([b1, b2, b3, b1, b2, b1], axis=0)
    writes = []
    sums = None
    for b, at in enumerate(blocks):
        a1, a2, a3 = (parts_ref[at, i * N : (i + 1) * N] for i in range(3))
        high, low = cut(dot(jnp.concatenate([a3, a2, a1, a2, a1, a1], axis=1), right), 2)
        high_ref[at, :] = high
        low_ref[at, :] = low
        for i, (source, target) in enumerate(((high_ref, high_out), (low_ref, low_out))):
            writes.append(pltpu.make_async_copy(source.at[at, :], target.at[at, :], out_sems.at[2 * b + i]))
            writes[-1].start()
        gain = dot(high.T, jnp.concatenate([high, low], axis=1))
        sums = gain if sums is None else sums + gain
    mixed = sums[:, N:]
    gram = sums[:, :N] + (mixed + mixed.T)
    packed_ref[0:64, :] = gram[0:64, :]
    packed_ref[64:128, :] = gram[64:128, :]
    packed_ref[64:128, 0:64] = pltpu.roll(gram[192:256, 128:256], 64, 1)[:, 0:64]
    packed_ref[128:160, 0:128] = gram[160:192, 128:256]
    packed_ref[128:160, 128:256] = gram[128:160, 128:256]
    for write in writes:
        write.wait()


def eliminate_panel(m_ref, r_ref, p):
    base = p * PANEL
    groups = PANEL // SUB
    lane = iota((SUB, N), 1)
    sub = iota((SUB, N), 0)
    sub1 = iota((SUB, 128), 0)
    for t in range(groups):
        top = base + t * SUB
        cols = []
        for k in range(SUB):
            cols.append([
                jnp.broadcast_to(m_ref[base + g * SUB : base + (g + 1) * SUB, top + k : top + k + 1], (SUB, 128))
                for g in range(t, groups)
            ])
        s = {}
        for k in range(SUB):
            for i in range(k, SUB):
                s[i, k] = jnp.broadcast_to(cols[k][0][i : i + 1, :], (SUB, 128))
        scale = []
        low = {}
        for k in range(SUB):
            r = lax.rsqrt(s[k, k])
            scale.append(r)
            for i in range(k + 1, SUB):
                low[i, k] = s[i, k] * r
            for j in range(k + 1, SUB):
                for i in range(j, SUB):
                    s[i, j] = s[i, j] - low[i, k] * low[j, k]
            for g in range(1, groups - t):
                cols[k][g] = cols[k][g] * r
                for j in range(k + 1, SUB):
                    cols[j][g] = cols[j][g] - cols[k][g] * low[j, k]
        half = top // 128
        own = slice(128 * half, 128 * (half + 1))
        lane_own = iota((SUB, 128), 1) + 128 * half
        rows = []
        twin = []
        for k in range(SUB):
            full = jnp.broadcast_to(m_ref[top + k : top + k + 1, :], (SUB, N))
            part = jnp.where(
                (lane_own >= top) & (lane_own < top + SUB),
                jnp.where(lane_own == top + k, 1.0, 0.0),
                full[:, own],
            )
            for j in range(k):
                c = low[k, j]
                full = full - jnp.concatenate([c, c], axis=1) * rows[j]
                part = part - c * twin[j]
            r = scale[k]
            rows.append(full * jnp.concatenate([r, r], axis=1))
            twin.append(part * r)
        w_true = rows[0]
        w_own = twin[0]
        for k in range(1, SUB):
            w_true = jnp.where(sub == k, rows[k], w_true)
            w_own = jnp.where(sub1 == k, twin[k], w_own)
        r_ref[top : top + SUB, :] = jnp.where(lane >= top + sub, w_true, 0.0)
        w_parts = [w_true[:, :128], w_true[:, 128:]]
        w_parts[half] = w_own
        m_ref[top : top + SUB, :] = jnp.concatenate(w_parts, axis=1)
        for g in range(1, groups - t):
            at = slice(base + (t + g) * SUB, base + (t + g + 1) * SUB)
            for h in range(2):
                old = m_ref[at, 128 * h : 128 * (h + 1)]
                if h == half:
                    old = jnp.where((lane_own >= top) & (lane_own < top + SUB), 0.0, old)
                total = None
                for k in range(SUB):
                    row = twin[k] if h == half else rows[k][:, 128 * h : 128 * (h + 1)]
                    term = cols[k][g] * row
                    total = term if total is None else total + term
                m_ref[at, 128 * h : 128 * (h + 1)] = old - total


def factor(m_ref, r_ref):
    for p in range(N // PANEL):
        eliminate_panel(m_ref, r_ref, p)
        base, below = p * PANEL, (p + 1) * PANEL
        if below < N:
            w = m_ref[base:below, :]
            lane = iota((PANEL, N), 1)
            ahead = (lane < below) & (lane > base + iota((PANEL, N), 0))
            gain = mm(w[:, below:] if below % 128 == 0 else w, jnp.where(ahead, 0.0, w), ((0,), (0,)))
            if below % 128:
                gain = gain[below:, :]
            lane = iota((N - below, N), 1)
            old = jnp.where((lane >= base) & (lane < below), 0.0, m_ref[below:, :])
            m_ref[below:, :] = old - gain


def second_kernel(row_scale, packed_ref, prior_ref, high_ref, low_ref, r_out, q_out, m_ref, r_ref, q_ref, sems):
    m_ref[0:64, :] = packed_ref[0:64, :]
    second = packed_ref[64:128, :]
    m_ref[64:128, :] = second
    m_ref[128:160, 128:256] = packed_ref[128:160, 128:256]
    m_ref[160:192, 128:256] = packed_ref[128:160, 0:128]
    m_ref[192:256, 128:256] = pltpu.roll(second[:, 0:128], 64, 1)
    m_ref[128:256, 0:128] = jnp.zeros((128, 128), F32)
    row_all, col_all = iota((N, N), 0), iota((N, N), 1)
    m_ref[...] = jnp.where(
        row_all // PANEL <= col_all // PANEL,
        m_ref[...] + jnp.where(row_all == col_all, 1.0, 0.0),
        0.0,
    )
    factor(m_ref, r_ref)
    b1, b2 = cut(jnp.where(row_all >= col_all, m_ref[...], 0.0).T * row_scale, 2)
    right = jnp.concatenate([b1, b2, b1], axis=0)
    copies = []
    for b in range(high_ref.shape[0] // BLOCK):
        at = slice(b * BLOCK, (b + 1) * BLOCK)
        high = high_ref[at, :]
        q_ref[at, :] = dot(jnp.concatenate([low_ref[at, :], high, high], axis=1), right)
        copies.append(
            pltpu.make_async_copy(
                q_ref.at[pl.ds(b * BLOCK, BLOCK), :], q_out.at[pl.ds(b * BLOCK, BLOCK), :], sems.at[b]
            )
        )
        copies[-1].start()
    r_out[...] = mm(r_ref[...], prior_ref[...]) * (1.0 / row_scale)
    for copy in copies:
        copy.wait()


def swap(value, axis, pairs):
    return lax.ppermute(value, axis, [p for a, b in pairs for p in ((a, b), (b, a))])


RING4 = (((0, 1), (2, 3)), ((1, 2), (3, 0)))
RING8 = (((0, 1), (2, 3), (4, 5), (6, 7)), ((1, 2), (3, 4), (5, 6), (7, 0)), ((0, 3), (1, 6), (2, 5), (4, 7)))


def sum_all(packed):
    one = lax.axis_index("core") == 1
    half = packed.shape[0] // 2
    first, last = packed[:half], packed[half:]
    mine = jnp.where(one, last, first) + swap(jnp.where(one, first, last), "core", ((0, 1),))
    for axis, turns in (("x", RING4), ("y", RING4), ("z", RING8)):
        for pairs in turns:
            mine = mine + swap(mine, axis, pairs)
    other = swap(mine, "core", ((0, 1),))
    return jnp.concatenate([jnp.where(one, other, mine), jnp.where(one, mine, other)], axis=0)


VMEM = pl.BlockSpec(memory_space=pltpu.VMEM)
HBM = pl.BlockSpec(memory_space=pltpu.HBM)
SMEM = pl.BlockSpec(memory_space=pltpu.SMEM)
PARAMS = pltpu.CompilerParams(vmem_limit_bytes=40 * 2**20)
FIRST = pltpu.CompilerParams(vmem_limit_bytes=60 * 2**20)


def stage_one(span, prior, counts):
    rows = span.shape[0]
    return pl.pallas_call(
        first_kernel,
        out_shape=(
            jax.ShapeDtypeStruct((rows, N), BF16),
            jax.ShapeDtypeStruct((rows, N), BF16),
            jax.ShapeDtypeStruct((160, N), F32),
        ),
        in_specs=[SMEM, HBM, VMEM],
        out_specs=(HBM, HBM, VMEM),
        scratch_shapes=[
            pltpu.VMEM((rows, N), F32),
            pltpu.VMEM((rows, 3 * N), BF16),
            pltpu.VMEM((rows, N), BF16),
            pltpu.VMEM((rows, N), BF16),
            pltpu.SemaphoreType.DMA((rows // BLOCK,)),
            pltpu.SemaphoreType.DMA((2 * rows // BLOCK,)),
        ],
        compiler_params=FIRST,
    )(counts, span, prior)


def stage_two(packed, prior, high, low, row_scale):
    rows = high.shape[0]
    return pl.pallas_call(
        functools.partial(second_kernel, row_scale),
        out_shape=(jax.ShapeDtypeStruct((N, N), F32), jax.ShapeDtypeStruct((rows, N), F32)),
        in_specs=[VMEM, VMEM, VMEM, VMEM],
        out_specs=(VMEM, HBM),
        scratch_shapes=[
            pltpu.VMEM((N, N), F32),
            pltpu.VMEM((N, N), F32),
            pltpu.VMEM((rows, N), F32),
            pltpu.SemaphoreType.DMA((rows // BLOCK,)),
        ],
        compiler_params=PARAMS,
    )(packed, prior, high, low)


def per_device(span, prior, counts, row_scale):
    high, low, packed = stage_one(span, prior, counts)
    return stage_two(sum_all(packed), prior, high, low, row_scale)


def solution(mesh):
    fine = Mesh(mesh.devices.reshape(4, 2, 4, 8), ("x", "core", "y", "z"))
    split = ("x", "core", "y", "z")

    def run(span, prior, counts):
        row_scale = math.sqrt(span.shape[0])
        return jax.shard_map(
            functools.partial(per_device, row_scale=row_scale),
            mesh=fine,
            in_specs=(P(split, None), P(), P(split)),
            out_specs=(P(), P(split, None)),
            check_vma=False,
        )(span, prior, counts)

    return run
```

```python
import functools
import math

import jax
import jax.numpy as jnp
from jax import lax
from jax.experimental import pallas as pl
from jax.experimental.pallas import tpu as pltpu
from jax.sharding import Mesh, PartitionSpec as P

F32 = jnp.float32
BF16 = jnp.bfloat16
BLOCK = 512
exact = lax.Precision.HIGHEST
N = 256
SUB = 8
PANEL = 64


def mm(a, b, dims=((1,), (0,))):
    return lax.dot_general(a, b, (dims, ((), ())), precision=exact, preferred_element_type=F32)


def cut(x, parts):
    out = []
    for _ in range(parts):
        out.append(x.astype(BF16))
        x = x - out[-1].astype(F32)
    return out


def dot(a, b, dims=((1,), (0,))):
    return lax.dot_general(a, b, (dims, ((), ())), preferred_element_type=F32)


def mm6(left, right):
    a1, a2, a3 = left
    b1, b2, b3 = right
    return dot(jnp.concatenate([a3, a2, a1, a2, a1, a1], axis=1), jnp.concatenate([b1, b2, b3, b1, b2, b1], axis=0))


def iota(shape, dim):
    return lax.broadcasted_iota(jnp.int32, shape, dim)


def lane_group_copy(x, k):
    half = x.shape[1] // 128
    out = []
    for h in range(half):
        part = x[:, 128 * h : 128 * (h + 1)]
        idx = (iota(part.shape, 1) // SUB) * SUB + k
        out.append(jnp.take_along_axis(part, idx, axis=1))
    return jnp.concatenate(out, axis=1)


def small_inverses(p_ref):
    lane = iota((SUB, N), 1)
    sub = iota((SUB, N), 0)
    diag = jnp.zeros((SUB, N), F32)
    for b in range(N // SUB):
        diag = jnp.where(lane // SUB == b, p_ref[SUB * b : SUB * (b + 1), :], diag)
    rest = jnp.where(lane % SUB == sub, 1.0, 0.0)
    small = jnp.zeros((SUB, N), F32)
    for k in reversed(range(SUB)):
        column = lane_group_copy(diag, k)
        row = jnp.broadcast_to(rest[k : k + 1, :] / column[k : k + 1, :], (SUB, N))
        small = jnp.where(sub == k, row, small)
        if k:
            rest = rest - jnp.where(sub < k, column, 0.0) * row
    return small


def upper_inverse(p_ref, small):
    half = N // 2
    row, col = iota((half, half), 0), iota((half, half), 1)
    corners = []
    for h in range(2):
        part = slice(half * h, half * (h + 1))
        inverse = jnp.where(row // SUB == col // SUB, jnp.concatenate([small[:, part]] * (half // SUB), axis=0), 0.0)
        upper = p_ref[part, part]
        size = SUB
        while size < half:
            pair = (row // (2 * size) == col // (2 * size)) & (row // size < col // size)
            known = cut(inverse, 3)
            inverse = inverse - mm6(known, cut(mm6(cut(jnp.where(pair, upper, 0.0), 3), known), 3))
            size *= 2
        corners.append(inverse)
    known = [cut(c, 3) for c in corners]
    cross = mm6(known[0], cut(mm6(cut(p_ref[:half, half:], 3), known[1]), 3))
    top = jnp.concatenate([corners[0], -cross], axis=1)
    return jnp.concatenate([top, jnp.concatenate([jnp.zeros((half, half), F32), corners[1]], axis=1)], axis=0)


def first_kernel(
    counts_ref, span_ref, prior_ref, high_out, low_out, packed_ref, rows_ref, parts_ref, high_ref, low_ref, in_sems, out_sems
):
    live = counts_ref[0]
    count = span_ref.shape[0] // BLOCK
    blocks = [pl.ds(b * BLOCK, BLOCK) for b in range(count)]
    copies = [pltpu.make_async_copy(span_ref.at[at, :], rows_ref.at[at, :], in_sems.at[b]) for b, at in enumerate(blocks)]
    for copy in copies:
        copy.start()
    small = small_inverses(prior_ref)
    for copy in copies:
        copy.wait()
    for b, at in enumerate(blocks):
        keep = iota((BLOCK, N), 0) + b * BLOCK < live
        for i, part in enumerate(cut(jnp.where(keep, rows_ref[at, :], 0.0), 3)):
            parts_ref[at, i * N : (i + 1) * N] = part
    b1, b2, b3 = cut(upper_inverse(prior_ref, small), 3)
    right = jnp.concatenate([b1, b2, b3, b1, b2, b1], axis=0)
    writes = []
    sums = None
    for b, at in enumerate(blocks):
        a1, a2, a3 = (parts_ref[at, i * N : (i + 1) * N] for i in range(3))
        high, low = cut(dot(jnp.concatenate([a3, a2, a1, a2, a1, a1], axis=1), right), 2)
        high_ref[at, :] = high
        low_ref[at, :] = low
        for i, (source, target) in enumerate(((high_ref, high_out), (low_ref, low_out))):
            writes.append(pltpu.make_async_copy(source.at[at, :], target.at[at, :], out_sems.at[2 * b + i]))
            writes[-1].start()
        gain = dot(high.T, jnp.concatenate([high, low], axis=1))
        sums = gain if sums is None else sums + gain
    mixed = sums[:, N:]
    gram = sums[:, :N] + (mixed + mixed.T)
    packed_ref[0:64, :] = gram[0:64, :]
    packed_ref[64:128, :] = gram[64:128, :]
    packed_ref[64:128, 0:64] = pltpu.roll(gram[192:256, 128:256], 64, 1)[:, 0:64]
    packed_ref[128:160, 0:128] = gram[160:192, 128:256]
    packed_ref[128:160, 128:256] = gram[128:160, 128:256]
    for write in writes:
        write.wait()


def spread(ref, row, col):
    return jnp.broadcast_to(ref[row : row + SUB, col : col + 1], (SUB, 128))


def eliminate_panel(m_ref, r_ref, p):
    base = p * PANEL
    groups = PANEL // SUB
    lane = iota((SUB, N), 1)
    sub = iota((SUB, N), 0)
    sub1 = iota((SUB, 128), 0)
    ahead = None
    for t in range(groups):
        top = base + t * SUB
        cols = [
            [
                ahead[k] if g == t and ahead else spread(m_ref, base + g * SUB, top + k)
                for g in range(t, groups)
            ]
            for k in range(SUB)
        ]
        scale = []
        low = {}
        for k in range(SUB):
            r = lax.rsqrt(jnp.broadcast_to(cols[k][0][k : k + 1, :], (SUB, 128)))
            scale.append(r)
            cols[k] = [c * r for c in cols[k]]
            for j in range(k + 1, SUB):
                low[j, k] = jnp.broadcast_to(cols[k][0][j : j + 1, :], (SUB, 128))
                cols[j] = [c - d * low[j, k] for c, d in zip(cols[j], cols[k])]
        if t + 1 < groups:
            ahead = []
            for j in range(SUB):
                block = spread(m_ref, top + SUB, top + SUB + j)
                for k in range(SUB):
                    block = block - cols[k][1] * jnp.broadcast_to(cols[k][1][j : j + 1, :], (SUB, 128))
                ahead.append(block)
        half = top // 128
        own = slice(128 * half, 128 * (half + 1))
        lane_own = iota((SUB, 128), 1) + 128 * half
        rows = []
        twin = []
        for k in range(SUB):
            full = jnp.broadcast_to(m_ref[top + k : top + k + 1, :], (SUB, N))
            part = jnp.where(
                (lane_own >= top) & (lane_own < top + SUB),
                jnp.where(lane_own == top + k, 1.0, 0.0),
                full[:, own],
            )
            for j in range(k):
                c = low[k, j]
                full = full - jnp.concatenate([c, c], axis=1) * rows[j]
                part = part - c * twin[j]
            r = scale[k]
            rows.append(full * jnp.concatenate([r, r], axis=1))
            twin.append(part * r)
        w_true = rows[0]
        w_own = twin[0]
        for k in range(1, SUB):
            w_true = jnp.where(sub == k, rows[k], w_true)
            w_own = jnp.where(sub1 == k, twin[k], w_own)
        r_ref[top : top + SUB, :] = jnp.where(lane >= top + sub, w_true, 0.0)
        w_parts = [w_true[:, :128], w_true[:, 128:]]
        w_parts[half] = w_own
        m_ref[top : top + SUB, :] = jnp.concatenate(w_parts, axis=1)
        for g in range(1, groups - t):
            at = slice(base + (t + g) * SUB, base + (t + g + 1) * SUB)
            for h in range(2):
                old = m_ref[at, 128 * h : 128 * (h + 1)]
                if h == half:
                    old = jnp.where((lane_own >= top) & (lane_own < top + SUB), 0.0, old)
                total = None
                for k in range(SUB):
                    row = twin[k] if h == half else rows[k][:, 128 * h : 128 * (h + 1)]
                    term = cols[k][g] * row
                    total = term if total is None else total + term
                m_ref[at, 128 * h : 128 * (h + 1)] = old - total


def factor(m_ref, r_ref):
    for p in range(N // PANEL):
        eliminate_panel(m_ref, r_ref, p)
        base, below = p * PANEL, (p + 1) * PANEL
        if below < N:
            w = m_ref[base:below, :]
            lane = iota((PANEL, N), 1)
            ahead = (lane < below) & (lane > base + iota((PANEL, N), 0))
            a1, a2, a3 = cut(w[:, 128:] if below >= 128 else w, 3)
            b1, b2, b3 = cut(jnp.where(ahead, 0.0, w), 3)
            gain = dot(
                jnp.concatenate([a3, a2, a1, a2, a1, a1], axis=0),
                jnp.concatenate([b1, b2, b3, b1, b2, b1], axis=0),
                ((0,), (0,)),
            )
            if below % 128:
                gain = gain[64:, :]
            lane = iota((N - below, N), 1)
            old = jnp.where((lane >= base) & (lane < below), 0.0, m_ref[below:, :])
            m_ref[below:, :] = old - gain


def second_kernel(row_scale, packed_ref, prior_ref, high_ref, low_ref, r_out, q_out, m_ref, r_ref, q_ref, sems):
    m_ref[0:64, :] = packed_ref[0:64, :]
    second = packed_ref[64:128, :]
    m_ref[64:128, :] = second
    m_ref[128:160, 128:256] = packed_ref[128:160, 128:256]
    m_ref[160:192, 128:256] = packed_ref[128:160, 0:128]
    m_ref[192:256, 128:256] = pltpu.roll(second[:, 0:128], 64, 1)
    m_ref[128:256, 0:128] = jnp.zeros((128, 128), F32)
    row_all, col_all = iota((N, N), 0), iota((N, N), 1)
    m_ref[...] = jnp.where(
        row_all // PANEL <= col_all // PANEL,
        m_ref[...] + jnp.where(row_all == col_all, 1.0, 0.0),
        0.0,
    )
    factor(m_ref, r_ref)
    b1, b2 = cut(jnp.where(row_all >= col_all, m_ref[...], 0.0).T * row_scale, 2)
    right = jnp.concatenate([b1, b2, b1], axis=0)
    copies = []
    for b in range(high_ref.shape[0] // BLOCK):
        at = slice(b * BLOCK, (b + 1) * BLOCK)
        high = high_ref[at, :]
        q_ref[at, :] = dot(jnp.concatenate([low_ref[at, :], high, high], axis=1), right)
        copies.append(
            pltpu.make_async_copy(
                q_ref.at[pl.ds(b * BLOCK, BLOCK), :], q_out.at[pl.ds(b * BLOCK, BLOCK), :], sems.at[b]
            )
        )
        copies[-1].start()
    r_out[...] = mm(r_ref[...], prior_ref[...]) * (1.0 / row_scale)
    for copy in copies:
        copy.wait()


def swap(value, axis, pairs):
    return lax.ppermute(value, axis, [p for a, b in pairs for p in ((a, b), (b, a))])


RING4 = (((0, 1), (2, 3)), ((1, 2), (3, 0)))
RING8 = (((0, 1), (2, 3), (4, 5), (6, 7)), ((1, 2), (3, 4), (5, 6), (7, 0)), ((0, 3), (1, 6), (2, 5), (4, 7)))


def sum_all(packed):
    one = lax.axis_index("core") == 1
    half = packed.shape[0] // 2
    first, last = packed[:half], packed[half:]
    mine = jnp.where(one, last, first) + swap(jnp.where(one, first, last), "core", ((0, 1),))
    for axis, turns in (("x", RING4), ("y", RING4), ("z", RING8)):
        for pairs in turns:
            mine = mine + swap(mine, axis, pairs)
    other = swap(mine, "core", ((0, 1),))
    return jnp.concatenate([jnp.where(one, other, mine), jnp.where(one, mine, other)], axis=0)


VMEM = pl.BlockSpec(memory_space=pltpu.VMEM)
HBM = pl.BlockSpec(memory_space=pltpu.HBM)
SMEM = pl.BlockSpec(memory_space=pltpu.SMEM)
PARAMS = pltpu.CompilerParams(vmem_limit_bytes=40 * 2**20)
FIRST = pltpu.CompilerParams(vmem_limit_bytes=50 * 2**20)


def stage_one(span, prior, counts):
    rows = span.shape[0]
    return pl.pallas_call(
        first_kernel,
        out_shape=(
            jax.ShapeDtypeStruct((rows, N), BF16),
            jax.ShapeDtypeStruct((rows, N), BF16),
            jax.ShapeDtypeStruct((160, N), F32),
        ),
        in_specs=[SMEM, HBM, VMEM],
        out_specs=(HBM, HBM, VMEM),
        scratch_shapes=[
            pltpu.VMEM((rows, N), F32),
            pltpu.VMEM((rows, 3 * N), BF16),
            pltpu.VMEM((rows, N), BF16),
            pltpu.VMEM((rows, N), BF16),
            pltpu.SemaphoreType.DMA((rows // BLOCK,)),
            pltpu.SemaphoreType.DMA((2 * rows // BLOCK,)),
        ],
        compiler_params=FIRST,
    )(counts, span, prior)


def stage_two(packed, prior, high, low, row_scale):
    rows = high.shape[0]
    return pl.pallas_call(
        functools.partial(second_kernel, row_scale),
        out_shape=(jax.ShapeDtypeStruct((N, N), F32), jax.ShapeDtypeStruct((rows, N), F32)),
        in_specs=[VMEM, VMEM, VMEM, VMEM],
        out_specs=(VMEM, HBM),
        scratch_shapes=[
            pltpu.VMEM((N, N), F32),
            pltpu.VMEM((N, N), F32),
            pltpu.VMEM((rows, N), F32),
            pltpu.SemaphoreType.DMA((rows // BLOCK,)),
        ],
        compiler_params=PARAMS,
    )(packed, prior, high, low)


def per_device(span, prior, counts, row_scale):
    high, low, packed = stage_one(span, prior, counts)
    return stage_two(sum_all(packed), prior, high, low, row_scale)


def solution(mesh):
    fine = Mesh(mesh.devices.reshape(4, 2, 4, 8), ("x", "core", "y", "z"))
    split = ("x", "core", "y", "z")

    def run(span, prior, counts):
        row_scale = math.sqrt(span.shape[0])
        return jax.shard_map(
            functools.partial(per_device, row_scale=row_scale),
            mesh=fine,
            in_specs=(P(split, None), P(), P(split)),
            out_specs=(P(), P(split, None)),
            check_vma=False,
        )(span, prior, counts)

    return run
```

```python
import functools
import math

import jax
import jax.numpy as jnp
from jax import lax
from jax.experimental import pallas as pl
from jax.experimental.pallas import tpu as pltpu
from jax.sharding import Mesh, PartitionSpec as P

F32 = jnp.float32
BF16 = jnp.bfloat16
BLOCK = 512
exact = lax.Precision.HIGHEST
N = 256
SUB = 8
PANEL = 64


def mm(a, b, dims=((1,), (0,))):
    return lax.dot_general(a, b, (dims, ((), ())), precision=exact, preferred_element_type=F32)


def cut(x, parts):
    out = []
    for _ in range(parts):
        out.append(x.astype(BF16))
        x = x - out[-1].astype(F32)
    return out


def dot(a, b, dims=((1,), (0,))):
    return lax.dot_general(a, b, (dims, ((), ())), preferred_element_type=F32)


def mm6(left, right):
    a1, a2, a3 = left
    b1, b2, b3 = right
    return dot(jnp.concatenate([a3, a2, a1, a2, a1, a1], axis=1), jnp.concatenate([b1, b2, b3, b1, b2, b1], axis=0))


def iota(shape, dim):
    return lax.broadcasted_iota(jnp.int32, shape, dim)


def lane_group_copy(x, k):
    half = x.shape[1] // 128
    out = []
    for h in range(half):
        part = x[:, 128 * h : 128 * (h + 1)]
        idx = (iota(part.shape, 1) // SUB) * SUB + k
        out.append(jnp.take_along_axis(part, idx, axis=1))
    return jnp.concatenate(out, axis=1)


def small_inverses(p_ref):
    lane = iota((SUB, N), 1)
    sub = iota((SUB, N), 0)
    diag = jnp.zeros((SUB, N), F32)
    for b in range(N // SUB):
        diag = jnp.where(lane // SUB == b, p_ref[SUB * b : SUB * (b + 1), :], diag)
    rest = jnp.where(lane % SUB == sub, 1.0, 0.0)
    small = jnp.zeros((SUB, N), F32)
    for k in reversed(range(SUB)):
        column = lane_group_copy(diag, k)
        row = jnp.broadcast_to(rest[k : k + 1, :] / column[k : k + 1, :], (SUB, N))
        small = jnp.where(sub == k, row, small)
        if k:
            rest = rest - jnp.where(sub < k, column, 0.0) * row
    return small


def upper_inverse(p_ref, small):
    half = N // 2
    row, col = iota((half, half), 0), iota((half, half), 1)
    corners = []
    for h in range(2):
        part = slice(half * h, half * (h + 1))
        inverse = jnp.where(row // SUB == col // SUB, jnp.concatenate([small[:, part]] * (half // SUB), axis=0), 0.0)
        upper = p_ref[part, part]
        size = SUB
        while size < half:
            pair = (row // (2 * size) == col // (2 * size)) & (row // size < col // size)
            known = cut(inverse, 3)
            inverse = inverse - mm6(known, cut(mm6(cut(jnp.where(pair, upper, 0.0), 3), known), 3))
            size *= 2
        corners.append(inverse)
    known = [cut(c, 3) for c in corners]
    cross = mm6(known[0], cut(mm6(cut(p_ref[:half, half:], 3), known[1]), 3))
    top = jnp.concatenate([corners[0], -cross], axis=1)
    return jnp.concatenate([top, jnp.concatenate([jnp.zeros((half, half), F32), corners[1]], axis=1)], axis=0)


def first_kernel(
    counts_ref, span_ref, prior_ref, high_out, low_out, packed_ref, rows_ref, parts_ref, high_ref, low_ref, in_sems, out_sems
):
    live = counts_ref[0]
    count = span_ref.shape[0] // BLOCK
    blocks = [pl.ds(b * BLOCK, BLOCK) for b in range(count)]
    copies = [pltpu.make_async_copy(span_ref.at[at, :], rows_ref.at[at, :], in_sems.at[b]) for b, at in enumerate(blocks)]
    for copy in copies:
        copy.start()
    small = small_inverses(prior_ref)
    for copy in copies:
        copy.wait()
    for b, at in enumerate(blocks):
        keep = iota((BLOCK, N), 0) + b * BLOCK < live
        for i, part in enumerate(cut(jnp.where(keep, rows_ref[at, :], 0.0), 3)):
            parts_ref[at, i * N : (i + 1) * N] = part
    b1, b2, b3 = cut(upper_inverse(prior_ref, small), 3)
    right = jnp.concatenate([b1, b2, b3, b1, b2, b1], axis=0)
    writes = []
    for b, at in enumerate(blocks):
        a1, a2, a3 = (parts_ref[at, i * N : (i + 1) * N] for i in range(3))
        high, low = cut(dot(jnp.concatenate([a3, a2, a1, a2, a1, a1], axis=1), right), 2)
        high_ref[at, :] = high
        low_ref[at, :] = low
        for i, (source, target) in enumerate(((high_ref, high_out), (low_ref, low_out))):
            writes.append(pltpu.make_async_copy(source.at[at, :], target.at[at, :], out_sems.at[2 * b + i]))
            writes[-1].start()
    sums = dot(high_ref[...], jnp.concatenate([high_ref[...], low_ref[...]], axis=1), ((0,), (0,)))
    mixed = sums[:, N:]
    gram = sums[:, :N] + (mixed + mixed.T)
    packed_ref[0:64, :] = gram[0:64, :]
    packed_ref[64:128, :] = gram[64:128, :]
    packed_ref[64:128, 0:64] = pltpu.roll(gram[192:256, 128:256], 64, 1)[:, 0:64]
    packed_ref[128:160, 0:128] = gram[160:192, 128:256]
    packed_ref[128:160, 128:256] = gram[128:160, 128:256]
    for write in writes:
        write.wait()


def spread(ref, row, col):
    return jnp.broadcast_to(ref[row : row + SUB, col : col + 1], (SUB, 128))


def eliminate_panel(m_ref, r_ref, p):
    base = p * PANEL
    groups = PANEL // SUB
    lane = iota((SUB, N), 1)
    sub = iota((SUB, N), 0)
    sub1 = iota((SUB, 128), 0)
    ahead = None
    for t in range(groups):
        top = base + t * SUB
        cols = [
            [
                ahead[k] if g == t and ahead else spread(m_ref, base + g * SUB, top + k)
                for g in range(t, groups)
            ]
            for k in range(SUB)
        ]
        scale = []
        low = {}
        for k in range(SUB):
            r = lax.rsqrt(jnp.broadcast_to(cols[k][0][k : k + 1, :], (SUB, 128)))
            scale.append(r)
            cols[k] = [c * r for c in cols[k]]
            for j in range(k + 1, SUB):
                low[j, k] = jnp.broadcast_to(cols[k][0][j : j + 1, :], (SUB, 128))
                cols[j] = [c - d * low[j, k] for c, d in zip(cols[j], cols[k])]
        if t + 1 < groups:
            ahead = []
            for j in range(SUB):
                block = spread(m_ref, top + SUB, top + SUB + j)
                for k in range(SUB):
                    block = block - cols[k][1] * jnp.broadcast_to(cols[k][1][j : j + 1, :], (SUB, 128))
                ahead.append(block)
        half = top // 128
        own = slice(128 * half, 128 * (half + 1))
        lane_own = iota((SUB, 128), 1) + 128 * half
        rows = []
        twin = []
        for k in range(SUB):
            full = jnp.broadcast_to(m_ref[top + k : top + k + 1, :], (SUB, N))
            part = jnp.where(
                (lane_own >= top) & (lane_own < top + SUB),
                jnp.where(lane_own == top + k, 1.0, 0.0),
                full[:, own],
            )
            for j in range(k):
                c = low[k, j]
                full = full - jnp.concatenate([c, c], axis=1) * rows[j]
                part = part - c * twin[j]
            r = scale[k]
            rows.append(full * jnp.concatenate([r, r], axis=1))
            twin.append(part * r)
        w_true = rows[0]
        w_own = twin[0]
        for k in range(1, SUB):
            w_true = jnp.where(sub == k, rows[k], w_true)
            w_own = jnp.where(sub1 == k, twin[k], w_own)
        r_ref[top : top + SUB, :] = jnp.where(lane >= top + sub, w_true, 0.0)
        w_parts = [w_true[:, :128], w_true[:, 128:]]
        w_parts[half] = w_own
        m_ref[top : top + SUB, :] = jnp.concatenate(w_parts, axis=1)
        for g in range(1, groups - t):
            at = slice(base + (t + g) * SUB, base + (t + g + 1) * SUB)
            for h in range(2):
                old = m_ref[at, 128 * h : 128 * (h + 1)]
                if h == half:
                    old = jnp.where((lane_own >= top) & (lane_own < top + SUB), 0.0, old)
                total = None
                for k in range(SUB):
                    row = twin[k] if h == half else rows[k][:, 128 * h : 128 * (h + 1)]
                    term = cols[k][g] * row
                    total = term if total is None else total + term
                m_ref[at, 128 * h : 128 * (h + 1)] = old - total


def factor(m_ref, r_ref):
    for p in range(N // PANEL):
        eliminate_panel(m_ref, r_ref, p)
        base, below = p * PANEL, (p + 1) * PANEL
        if below < N:
            w = m_ref[base:below, :]
            lane = iota((PANEL, N), 1)
            ahead = (lane < below) & (lane > base + iota((PANEL, N), 0))
            a1, a2, a3 = cut(w[:, 128:] if below >= 128 else w, 3)
            b1, b2, b3 = cut(jnp.where(ahead, 0.0, w), 3)
            gain = dot(
                jnp.concatenate([a3, a2, a1, a2, a1, a1], axis=0),
                jnp.concatenate([b1, b2, b3, b1, b2, b1], axis=0),
                ((0,), (0,)),
            )
            if below % 128:
                gain = gain[64:, :]
            lane = iota((N - below, N), 1)
            old = jnp.where((lane >= base) & (lane < below), 0.0, m_ref[below:, :])
            m_ref[below:, :] = old - gain


def second_kernel(row_scale, packed_ref, prior_ref, high_ref, low_ref, r_out, q_out, m_ref, r_ref, q_ref, sems):
    m_ref[0:64, :] = packed_ref[0:64, :]
    second = packed_ref[64:128, :]
    m_ref[64:128, :] = second
    m_ref[128:160, 128:256] = packed_ref[128:160, 128:256]
    m_ref[160:192, 128:256] = packed_ref[128:160, 0:128]
    m_ref[192:256, 128:256] = pltpu.roll(second[:, 0:128], 64, 1)
    m_ref[128:256, 0:128] = jnp.zeros((128, 128), F32)
    row_all, col_all = iota((N, N), 0), iota((N, N), 1)
    m_ref[...] = jnp.where(
        row_all // PANEL <= col_all // PANEL,
        m_ref[...] + jnp.where(row_all == col_all, 1.0, 0.0),
        0.0,
    )
    factor(m_ref, r_ref)
    b1, b2 = cut(jnp.where(row_all >= col_all, m_ref[...], 0.0).T * row_scale, 2)
    right = jnp.concatenate([b1, b2, b1], axis=0)
    copies = []
    for b in range(high_ref.shape[0] // BLOCK):
        at = slice(b * BLOCK, (b + 1) * BLOCK)
        high = high_ref[at, :]
        q_ref[at, :] = dot(jnp.concatenate([low_ref[at, :], high, high], axis=1), right)
        copies.append(
            pltpu.make_async_copy(
                q_ref.at[pl.ds(b * BLOCK, BLOCK), :], q_out.at[pl.ds(b * BLOCK, BLOCK), :], sems.at[b]
            )
        )
        copies[-1].start()
    r_out[...] = mm(r_ref[...], prior_ref[...]) * (1.0 / row_scale)
    for copy in copies:
        copy.wait()


def swap(value, axis, pairs):
    return lax.ppermute(value, axis, [p for a, b in pairs for p in ((a, b), (b, a))])


RING4 = (((0, 1), (2, 3)), ((1, 2), (3, 0)))
RING8 = (((0, 1), (2, 3), (4, 5), (6, 7)), ((1, 2), (3, 4), (5, 6), (7, 0)), ((0, 3), (1, 6), (2, 5), (4, 7)))


def sum_all(packed):
    one = lax.axis_index("core") == 1
    half = packed.shape[0] // 2
    first, last = packed[:half], packed[half:]
    mine = jnp.where(one, last, first) + swap(jnp.where(one, first, last), "core", ((0, 1),))
    for axis, turns in (("x", RING4), ("y", RING4), ("z", RING8)):
        for pairs in turns:
            mine = mine + swap(mine, axis, pairs)
    other = swap(mine, "core", ((0, 1),))
    return jnp.concatenate([jnp.where(one, other, mine), jnp.where(one, mine, other)], axis=0)


VMEM = pl.BlockSpec(memory_space=pltpu.VMEM)
HBM = pl.BlockSpec(memory_space=pltpu.HBM)
SMEM = pl.BlockSpec(memory_space=pltpu.SMEM)
PARAMS = pltpu.CompilerParams(vmem_limit_bytes=40 * 2**20)
FIRST = pltpu.CompilerParams(vmem_limit_bytes=50 * 2**20)


def stage_one(span, prior, counts):
    rows = span.shape[0]
    return pl.pallas_call(
        first_kernel,
        out_shape=(
            jax.ShapeDtypeStruct((rows, N), BF16),
            jax.ShapeDtypeStruct((rows, N), BF16),
            jax.ShapeDtypeStruct((160, N), F32),
        ),
        in_specs=[SMEM, HBM, VMEM],
        out_specs=(HBM, HBM, VMEM),
        scratch_shapes=[
            pltpu.VMEM((rows, N), F32),
            pltpu.VMEM((rows, 3 * N), BF16),
            pltpu.VMEM((rows, N), BF16),
            pltpu.VMEM((rows, N), BF16),
            pltpu.SemaphoreType.DMA((rows // BLOCK,)),
            pltpu.SemaphoreType.DMA((2 * rows // BLOCK,)),
        ],
        compiler_params=FIRST,
    )(counts, span, prior)


def stage_two(packed, prior, high, low, row_scale):
    rows = high.shape[0]
    return pl.pallas_call(
        functools.partial(second_kernel, row_scale),
        out_shape=(jax.ShapeDtypeStruct((N, N), F32), jax.ShapeDtypeStruct((rows, N), F32)),
        in_specs=[VMEM, VMEM, VMEM, VMEM],
        out_specs=(VMEM, HBM),
        scratch_shapes=[
            pltpu.VMEM((N, N), F32),
            pltpu.VMEM((N, N), F32),
            pltpu.VMEM((rows, N), F32),
            pltpu.SemaphoreType.DMA((rows // BLOCK,)),
        ],
        compiler_params=PARAMS,
    )(packed, prior, high, low)


def per_device(span, prior, counts, row_scale):
    high, low, packed = stage_one(span, prior, counts)
    return stage_two(sum_all(packed), prior, high, low, row_scale)


def solution(mesh):
    fine = Mesh(mesh.devices.reshape(4, 2, 4, 8), ("x", "core", "y", "z"))
    split = ("x", "core", "y", "z")

    def run(span, prior, counts):
        row_scale = math.sqrt(span.shape[0])
        return jax.shard_map(
            functools.partial(per_device, row_scale=row_scale),
            mesh=fine,
            in_specs=(P(split, None), P(), P(split)),
            out_specs=(P(), P(split, None)),
            check_vma=False,
        )(span, prior, counts)

    return run
```
